1024 devices in a mesh: row: 32 (over z), col: 32 (over y, x, core).
Axes of the slice: x: 4, y: 4, z: 32, core: 2. Of those that a mesh axis runs over, the one named last changes fastest.
Arguments:
- features: bfloat16 [65536, 256], P(('col', 'row')), may hold values from -6 to 6
- block_rows: int32 [32, 32, 24], P('row', 'col'), may hold values from 0 to 15, as said below
- block_cols: int32 [32, 32, 24], P('row', 'col'), may hold values from 0 to 15
- block_values: bfloat16 [32, 32, 24, 128, 128], P('row', 'col'), may hold values from -0.078125 to 0.078125
- block_count: int32 [32, 32], P('row', 'col'), may hold values from 1 to 24, as said below
- w_first: bfloat16 [256, 256], replicated, may hold values from -0.375 to 0.375
- b_first: float32 [256], replicated, may hold values from -3 to 3
- w_second: bfloat16 [256, 256], replicated, may hold values from -0.375 to 0.375
- b_second: float32 [256], replicated, may hold values from -3 to 3
Outputs:
- embedded: bfloat16 [65536, 256], P(('col', 'row'))
The draws below stay inside these ranges and needn't reach their ends.
Inputs may be any that keep to these rules, and one draw needn't show every extreme that they name: Within each tile the slots hold distinct (block_rows, block_cols) pairs. Slots at or past block_count hold no part of A. Some tile in every draw has all 24 slots live.
All inputs are finite; a program needn't handle non-finite values.
Results may differ from the reference program's by a relative error of at most 0.0054.
Values may be sent and summed in bfloat16 or wider, within the bound.
No kernel may reach another device: no remote copies, remote signals or barrier semaphores. Data moves between devices by JAX's collectives and lax.ppermute only.
A program may use at most 32 MiB of HBM per device.

```python
import jax
import jax.numpy as jnp
from jax import lax

D = 256
BLK = 128
GR = 32
GC = 32
NODES = 65536
RR = 2048
CR = 2048
RBT = 16
CBT = 16
NNZ_DEV = 24


def slot_positions(key):
    device_keys = jax.random.split(key, GR * GC)
    chosen = jax.vmap(lambda one_key: jax.random.permutation(one_key, RBT * CBT)[:NNZ_DEV])(device_keys)
    return chosen.reshape(GR, GC, NNZ_DEV).astype(jnp.int32)


def draw_block_rows(key, part):
    return (slot_positions(key) // CBT).astype(jnp.int32)


def draw_block_cols(key, part):
    return (slot_positions(key) % CBT).astype(jnp.int32)


def draw_block_count(key, part):
    key = jax.random.fold_in(key, 7)
    first_key, second_key = jax.random.split(key)
    raw = jax.random.randint(first_key, (GR * GC,), 0, NNZ_DEV)
    counts = 1 + raw * raw // NNZ_DEV
    fullest = jax.random.randint(second_key, (), 0, GR * GC)
    counts = jnp.where(jnp.arange(GR * GC) == fullest, NNZ_DEV, counts)
    return jnp.minimum(counts, NNZ_DEV).reshape(GR, GC).astype(jnp.int32)


def block_scale(stream_key, dims, cuts, least, top_value):
    def one(position, shards_of):
        draws = jax.random.uniform(jax.random.fold_in(jax.random.fold_in(stream_key, 6), position), (shards_of,), jnp.float32, least / len(cuts), top_value / len(cuts))
        return jnp.repeat(jnp.exp(draws), dims[position] // shards_of).reshape((-1,) + (1,) * (len(dims) - position - 1))

    loudness = one(*cuts[0])
    for cut in cuts[1:]:
        loudness = loudness * one(*cut)
    return loudness


def gaussian(stream_key, dims, scale, most, cuts=(), held_as=jnp.bfloat16):
    drawn = scale * jax.random.normal(stream_key, dims, jnp.float32)
    if cuts:
        drawn = drawn * block_scale(stream_key, dims, cuts, -0.22, 0.18)
    return jnp.clip(drawn, -most, most).astype(held_as)


def setup_inputs(seed: int = 0) -> dict:
    key_of = jax.random.split(jax.random.key(seed), 10)
    features = gaussian(key_of[0], (NODES, D), 1.0, 6.0, ((0, 1024),))
    block_rows = draw_block_rows(jax.random.fold_in(key_of[9], 71), 0)
    block_cols = draw_block_cols(jax.random.fold_in(key_of[9], 71), 0)
    block_values = gaussian(key_of[3], (GR, GC, NNZ_DEV, BLK, BLK), (BLK * max(1, NNZ_DEV * GC // RBT)) ** -0.5, 0.078125, ((0, 32), (1, 32)))
    block_count = draw_block_count(jax.random.fold_in(key_of[9], 71), 0)
    w_first = gaussian(key_of[5], (D, D), D ** -0.5, 0.375)
    b_first = gaussian(key_of[6], (D,), 0.5, 3.0, (), jnp.float32)
    w_second = gaussian(key_of[7], (D, D), D ** -0.5, 0.375)
    b_second = gaussian(key_of[8], (D,), 0.5, 3.0, (), jnp.float32)
    return dict(features=features, block_rows=block_rows, block_cols=block_cols, block_values=block_values, block_count=block_count, w_first=w_first, b_first=b_first, w_second=w_second, b_second=b_second)


def tile_term(values, sel_idx, out_idx, out_blocks, count, panel, transpose):
    panel_tiles = panel.astype(jnp.float32).reshape(-1, BLK, D)
    picked = panel_tiles[sel_idx]
    pattern = "nji,njd->nid" if transpose else "nij,njd->nid"
    products = jnp.einsum(pattern, values.astype(jnp.float32), picked, precision=lax.Precision.HIGHEST)
    live_slots = jnp.arange(NNZ_DEV, dtype=jnp.int32) < count
    onehot = ((out_idx[None, :] == jnp.arange(out_blocks, dtype=jnp.int32)[:, None]) & live_slots[None, :]).astype(jnp.float32)
    summed = jnp.dot(onehot, products.reshape(NNZ_DEV, BLK * D), precision=lax.Precision.HIGHEST, preferred_element_type=jnp.float32)
    return summed.reshape(out_blocks * BLK, D)


def reference(features, block_rows, block_cols, block_values, block_count, w_first, b_first, w_second, b_second):
    def first_step(device, total):
        row_index = (device // GC).astype(jnp.int32)
        col_index = (device % GC).astype(jnp.int32)
        panel = lax.dynamic_slice_in_dim(features, (col_index * CR).astype(jnp.int32), CR, 0)
        term = tile_term(block_values[row_index, col_index], block_cols[row_index, col_index], block_rows[row_index, col_index], RBT, block_count[row_index, col_index], panel, False)
        start = (row_index * RR).astype(jnp.int32)
        current = lax.dynamic_slice_in_dim(total, start, RR, 0)
        return lax.dynamic_update_slice_in_dim(total, current + term, start, 0)

    agg_first = lax.fori_loop(0, GR * GC, first_step, jnp.zeros((NODES, D), jnp.float32)).astype(jnp.bfloat16)
    hidden = jax.nn.relu(jnp.dot(agg_first, w_first, preferred_element_type=jnp.float32) + b_first).astype(jnp.bfloat16)

    def second_step(device, total):
        row_index = (device // GC).astype(jnp.int32)
        col_index = (device % GC).astype(jnp.int32)
        panel = lax.dynamic_slice_in_dim(hidden, (row_index * RR).astype(jnp.int32), RR, 0)
        term = tile_term(block_values[row_index, col_index], block_rows[row_index, col_index], block_cols[row_index, col_index], CBT, block_count[row_index, col_index], panel, True)
        start = (col_index * CR).astype(jnp.int32)
        current = lax.dynamic_slice_in_dim(total, start, CR, 0)
        return lax.dynamic_update_slice_in_dim(total, current + term, start, 0)

    agg_second = lax.fori_loop(0, GR * GC, second_step, jnp.zeros((NODES, D), jnp.float32)).astype(jnp.bfloat16)
    return (jnp.dot(agg_second, w_second, preferred_element_type=jnp.float32) + b_second).astype(jnp.bfloat16)
```

```python
import functools

import jax
import jax.numpy as jnp
from jax import lax
from jax.experimental import pallas as pl
from jax.experimental.pallas import tpu as pltpu
from jax.sharding import PartitionSpec as P

ROW, COL = "row", "col"
BF16, F32 = jnp.bfloat16, jnp.float32
VMEM = pl.BlockSpec(memory_space=pltpu.VMEM)
SMEM = pl.BlockSpec(memory_space=pltpu.SMEM)
GROUP = 4
VMEM_LIMIT = 12 * 1024 * 1024
PLACE_ROW, PLACE_COL, COUNT, FIRST = 0, 1, 2, 3


def strided(size, stride):
    return [list(range(first, size, stride)) for first in range(stride)]


def shift(size, by):
    return [(i, (i + by) % size) for i in range(size)]


def hop_two(size):
    return [(i, (i + (2 if i % 2 == 0 else -2)) % size) for i in range(size)]


def swap(size):
    return [(i, i + 1 if i % 2 == 0 else i - 1) for i in range(size)]


def fill_panel(panel, own, other, side):
    half = own.shape[1]
    panel[:, pl.ds(pl.multiple_of(side * half, half), half), :] = own[...]
    panel[:, pl.ds(pl.multiple_of((1 - side) * half, half), half), :] = other[...]


def add_products(panel, acc, facts, from_at, to_at, values, transpose):
    spare = acc.shape[0] - 1
    slots = values.shape[0]
    live = facts[COUNT]
    contract = (((0,), (0,)), ((), ())) if transpose else (((1,), (0,)), ((), ()))

    def step(g, carry):
        base = g * GROUP
        products = [
            lax.dot_general(
                values[base + k], panel[facts[from_at + base + k]], contract, preferred_element_type=F32
            )
            for k in range(GROUP)
        ]
        for k in range(GROUP):
            to = jnp.where(base + k < live, facts[to_at + base + k], spare)
            acc[to] += products[k]
        return carry

    assert slots % GROUP == 0
    lax.fori_loop(0, (live + GROUP - 1) // GROUP, step, 0)


def keep_near_kernel(after, values, bias_0, bias_1, values_out, bias_0_out, bias_1_out):
    del after
    for source, target in ((values, values_out), (bias_0, bias_0_out), (bias_1, bias_1_out)):
        target[...] = source[...]


def first_kernel(facts, values, own, other, keep, send, panel, acc):
    fill_panel(panel, own, other, lax.rem(facts[PLACE_ROW], 2))
    acc[...] = jnp.zeros_like(acc)
    slots = values.shape[0]
    add_products(panel, acc, facts, FIRST + slots, FIRST, values, False)
    chips, half = keep.shape[:2]
    core = lax.rem(facts[PLACE_COL], 2)
    keep[...] = acc[:chips, pl.ds(pl.multiple_of(core * half, half), half), :]
    send[...] = acc[:chips, pl.ds(pl.multiple_of((1 - core) * half, half), half), :]


def second_kernel(facts, values, own, other, keep, up, down, two, panel, acc):
    fill_panel(panel, own, other, lax.rem(facts[PLACE_COL], 2))
    acc[...] = jnp.zeros_like(acc)
    slots = values.shape[0]
    add_products(panel, acc, facts, FIRST, FIRST + slots, values, True)
    quads, half = keep.shape[:2]
    for ref, by in ((keep, 0), (up, 1), (down, 3), (two, 2)):
        r = lax.rem(facts[PLACE_ROW] + by, 4)
        offset = pl.multiple_of(lax.rem(r, 2) * half, half)
        for k in range(quads):
            ref[k] = acc[2 * k + r // 2, pl.ds(offset, half), :].astype(ref.dtype)


def dense_kernel(layer, parts, weight, bias, out):
    total = jnp.sum(parts[...].astype(F32), axis=0).astype(BF16)
    result = jnp.dot(total, weight[...], preferred_element_type=F32) + bias[...]
    if layer == 0:
        result = jnp.maximum(result, 0.0)
    result = result.astype(BF16)
    if len(out.shape) == 3:
        for k in range(out.shape[0]):
            out[k] = result
    else:
        out[...] = result


def call(kernel, out_shape, in_specs, scratch=()):
    return pl.pallas_call(
        kernel,
        out_shape=out_shape,
        in_specs=in_specs,
        out_specs=jax.tree.map(lambda _: VMEM, out_shape),
        scratch_shapes=list(scratch),
        compiler_params=pltpu.CompilerParams(vmem_limit_bytes=VMEM_LIMIT),
    )


def shape(dims, dtype):
    return jax.ShapeDtypeStruct(dims, dtype)


def per_device(
    features,
    block_rows,
    block_cols,
    block_values,
    block_count,
    w_first,
    b_first,
    w_second,
    b_second,
):
    rows, cols = lax.axis_size(ROW), lax.axis_size(COL)
    own_rows, width = features.shape
    block = block_values.shape[-1]
    values = block_values[0, 0]
    row_blocks = own_rows * cols // block
    col_blocks = own_rows * rows // block
    scratch = (
        pltpu.VMEM((col_blocks, block, width), BF16),
        pltpu.VMEM((row_blocks + 1, block, width), F32),
    )
    place = jnp.stack([lax.axis_index(ROW), lax.axis_index(COL)]).astype(jnp.int32)
    facts = jnp.concatenate([place, block_count[0], block_rows[0, 0], block_cols[0, 0]])
    chips, quads = cols // 2, rows // 4

    same = lax.all_gather(features, ROW, axis_index_groups=strided(rows, 2))
    other = lax.ppermute(same, ROW, swap(rows))
    piece = (chips, own_rows, width)
    bias_shape = (1, width)
    near = (shape(values.shape, BF16), shape(bias_shape, F32), shape(bias_shape, F32))
    values, bias_first, bias_second = call(keep_near_kernel, near, [VMEM] * 4)(
        same, values, b_first.reshape(bias_shape), b_second.reshape(bias_shape)
    )
    keep, send = call(
        first_kernel, (shape(piece, F32), shape(piece, F32)), [SMEM] + [VMEM] * 3, scratch
    )(facts, values, same, other)

    summed = (keep + lax.ppermute(send, COL, swap(cols))).astype(BF16)
    terms = lax.all_to_all(summed, COL, 0, 0, axis_index_groups=strided(cols, 2))
    copies = call(functools.partial(dense_kernel, 0), shape(piece, BF16), [VMEM] * 3)(
        terms, w_first, bias_first
    )

    mine = lax.all_to_all(copies, COL, 0, 0, axis_index_groups=strided(cols, 2))
    other = lax.ppermute(mine, COL, swap(cols))
    piece = (quads, own_rows, width)
    keep, up, down, two = call(
        second_kernel,
        (shape(piece, F32), shape(piece, BF16), shape(piece, BF16), shape(piece, BF16)),
        [SMEM] + [VMEM] * 3,
        scratch,
    )(facts, values, mine, other)

    two = lax.ppermute(two, ROW, hop_two(rows))
    up = lax.ppermute(up, ROW, shift(rows, 1))
    down = lax.ppermute(down, ROW, shift(rows, -1))
    summed = (keep + up.astype(F32) + down.astype(F32) + two.astype(F32)).astype(BF16)
    terms = lax.all_to_all(summed, ROW, 0, 0, axis_index_groups=strided(rows, 4))
    return call(functools.partial(dense_kernel, 1), shape((own_rows, width), BF16), [VMEM] * 3)(
        terms, w_second, bias_second
    )


def solution(mesh):
    placed = (
        P((COL, ROW), None),
        P(ROW, COL, None),
        P(ROW, COL, None),
        P(ROW, COL, None, None, None),
        P(ROW, COL),
        P(),
        P(),
        P(),
        P(),
    )
    return jax.shard_map(
        per_device, mesh=mesh, in_specs=placed, out_specs=P((COL, ROW), None), check_vma=False
    )
```

```python
import functools

import jax
import jax.numpy as jnp
from jax import lax
from jax.experimental import pallas as pl
from jax.experimental.pallas import tpu as pltpu
from jax.sharding import PartitionSpec as P

ROW, COL = "row", "col"
BF16, F32 = jnp.bfloat16, jnp.float32
VMEM = pl.BlockSpec(memory_space=pltpu.VMEM)
SMEM = pl.BlockSpec(memory_space=pltpu.SMEM)
GROUP = 4
VMEM_LIMIT = 12 * 1024 * 1024
PLACE_ROW, PLACE_COL, COUNT, FIRST = 0, 1, 2, 3


def strided(size, stride):
    return [list(range(first, size, stride)) for first in range(stride)]


def shift(size, by):
    return [(i, (i + by) % size) for i in range(size)]


def hop_two(size):
    return [(i, (i + (2 if i % 2 == 0 else -2)) % size) for i in range(size)]


def swap(size):
    return [(i, i + 1 if i % 2 == 0 else i - 1) for i in range(size)]


def fill_panel(panel, own, other, side):
    half = own.shape[1]
    panel[:, pl.ds(pl.multiple_of(side * half, half), half), :] = own[...]
    panel[:, pl.ds(pl.multiple_of((1 - side) * half, half), half), :] = other[...]


def add_products(panel, acc, facts, from_at, to_at, values, transpose):
    spare = acc.shape[0] - 1
    slots = values.shape[0]
    live = facts[COUNT]
    contract = (((0,), (0,)), ((), ())) if transpose else (((1,), (0,)), ((), ()))

    def step(g, carry):
        base = g * GROUP
        products = [
            lax.dot_general(
                values[base + k], panel[facts[from_at + base + k]], contract, preferred_element_type=F32
            )
            for k in range(GROUP)
        ]
        for k in range(GROUP):
            to = jnp.where(base + k < live, facts[to_at + base + k], spare)
            acc[to] += products[k]
        return carry

    assert slots % GROUP == 0
    lax.fori_loop(0, (live + GROUP - 1) // GROUP, step, 0)


def keep_near_kernel(after, values, bias_0, bias_1, values_out, bias_0_out, bias_1_out):
    del after
    for source, target in ((values, values_out), (bias_0, bias_0_out), (bias_1, bias_1_out)):
        target[...] = source[...]


def first_kernel(facts, values, own, other, keep, send, panel, acc):
    fill_panel(panel, own, other, lax.rem(facts[PLACE_ROW], 2))
    acc[...] = jnp.zeros_like(acc)
    slots = values.shape[0]
    add_products(panel, acc, facts, FIRST + slots, FIRST, values, False)
    chips, half = keep.shape[:2]
    core = lax.rem(facts[PLACE_COL], 2)
    keep[...] = acc[:chips, pl.ds(pl.multiple_of(core * half, half), half), :]
    send[...] = acc[:chips, pl.ds(pl.multiple_of((1 - core) * half, half), half), :]


def second_kernel(facts, values, own, other, keep, two, up, down, panel, acc):
    fill_panel(panel, own, other, lax.rem(facts[PLACE_COL], 2))
    acc[...] = jnp.zeros_like(acc)
    slots = values.shape[0]
    add_products(panel, acc, facts, FIRST, FIRST + slots, values, True)
    quads, half = keep.shape[:2]
    for ref, by in ((two, 2), (up, 1), (down, 3), (keep, 0)):
        r = lax.rem(facts[PLACE_ROW] + by, 4)
        offset = pl.multiple_of(lax.rem(r, 2) * half, half)
        for k in range(quads):
            ref[k] = acc[2 * k + r // 2, pl.ds(offset, half), :].astype(ref.dtype)


def dense_kernel(layer, parts, weight, bias, out):
    total = jnp.sum(parts[...].astype(F32), axis=0).astype(BF16)
    result = jnp.dot(total, weight[...], preferred_element_type=F32) + bias[...]
    if layer == 0:
        result = jnp.maximum(result, 0.0)
    result = result.astype(BF16)
    if len(out.shape) == 3:
        for k in range(out.shape[0]):
            out[k] = result
    else:
        out[...] = result


def call(kernel, out_shape, in_specs, scratch=()):
    return pl.pallas_call(
        kernel,
        out_shape=out_shape,
        in_specs=in_specs,
        out_specs=jax.tree.map(lambda _: VMEM, out_shape),
        scratch_shapes=list(scratch),
        compiler_params=pltpu.CompilerParams(vmem_limit_bytes=VMEM_LIMIT),
    )


def shape(dims, dtype):
    return jax.ShapeDtypeStruct(dims, dtype)


def per_device(
    features,
    block_rows,
    block_cols,
    block_values,
    block_count,
    w_first,
    b_first,
    w_second,
    b_second,
):
    rows, cols = lax.axis_size(ROW), lax.axis_size(COL)
    own_rows, width = features.shape
    block = block_values.shape[-1]
    values = block_values[0, 0]
    row_blocks = own_rows * cols // block
    col_blocks = own_rows * rows // block
    scratch = (
        pltpu.VMEM((col_blocks, block, width), BF16),
        pltpu.VMEM((row_blocks + 1, block, width), F32),
    )
    place = jnp.stack([lax.axis_index(ROW), lax.axis_index(COL)]).astype(jnp.int32)
    facts = jnp.concatenate([place, block_count[0], block_rows[0, 0], block_cols[0, 0]])
    chips, quads = cols // 2, rows // 4

    same = lax.all_gather(features, ROW, axis_index_groups=strided(rows, 2))
    other = lax.ppermute(same, ROW, swap(rows))
    piece = (chips, own_rows, width)
    bias_shape = (1, width)
    near = (shape(values.shape, BF16), shape(bias_shape, F32), shape(bias_shape, F32))
    values, bias_first, bias_second = call(keep_near_kernel, near, [VMEM] * 4)(
        same, values, b_first.reshape(bias_shape), b_second.reshape(bias_shape)
    )
    keep, send = call(
        first_kernel, (shape(piece, F32), shape(piece, F32)), [SMEM] + [VMEM] * 3, scratch
    )(facts, values, same, other)

    summed = (keep + lax.ppermute(send, COL, swap(cols))).astype(BF16)
    terms = lax.all_to_all(summed, COL, 0, 0, axis_index_groups=strided(cols, 2))
    copies = call(functools.partial(dense_kernel, 0), shape(piece, BF16), [VMEM] * 3)(
        terms, w_first, bias_first
    )

    mine = lax.all_to_all(copies, COL, 0, 0, axis_index_groups=strided(cols, 2))
    other = lax.ppermute(mine, COL, swap(cols))
    piece = (quads, own_rows, width)
    keep, two, up, down = call(
        second_kernel,
        (shape(piece, F32), shape(piece, BF16), shape(piece, BF16), shape(piece, BF16)),
        [SMEM] + [VMEM] * 3,
        scratch,
    )(facts, values, mine, other)

    two = lax.ppermute(two, ROW, hop_two(rows))
    up = lax.ppermute(up, ROW, shift(rows, 1))
    down = lax.ppermute(down, ROW, shift(rows, -1))
    summed = (keep + two.astype(F32) + up.astype(F32) + down.astype(F32)).astype(BF16)
    terms = lax.all_to_all(summed, ROW, 0, 0, axis_index_groups=strided(rows, 4))
    return call(functools.partial(dense_kernel, 1), shape((own_rows, width), BF16), [VMEM] * 3)(
        terms, w_second, bias_second
    )


def solution(mesh):
    placed = (
        P((COL, ROW), None),
        P(ROW, COL, None),
        P(ROW, COL, None),
        P(ROW, COL, None, None, None),
        P(ROW, COL),
        P(),
        P(),
        P(),
        P(),
    )
    return jax.shard_map(
        per_device, mesh=mesh, in_specs=placed, out_specs=P((COL, ROW), None), check_vma=False
    )
```

```python
import functools

import jax
import jax.numpy as jnp
from jax import lax
from jax.experimental import pallas as pl
from jax.experimental.pallas import tpu as pltpu
from jax.sharding import PartitionSpec as P

ROW, COL = "row", "col"
BF16, F32 = jnp.bfloat16, jnp.float32
VMEM = pl.BlockSpec(memory_space=pltpu.VMEM)
SMEM = pl.BlockSpec(memory_space=pltpu.SMEM)
GROUP = 4
VMEM_LIMIT = 12 * 1024 * 1024
PLACE_ROW, PLACE_COL, COUNT, FIRST = 0, 1, 2, 3


def strided(size, stride):
    return [list(range(first, size, stride)) for first in range(stride)]


def shift(size, by):
    return [(i, (i + by) % size) for i in range(size)]


def hop_two(size):
    return [(i, (i + (2 if i % 2 == 0 else -2)) % size) for i in range(size)]


def swap(size):
    return [(i, i + 1 if i % 2 == 0 else i - 1) for i in range(size)]


def fill_panel(panel, own, other, side):
    half = own.shape[1]
    panel[:, pl.ds(pl.multiple_of(side * half, half), half), :] = own[...]
    panel[:, pl.ds(pl.multiple_of((1 - side) * half, half), half), :] = other[...]


def add_products(panel, acc, facts, from_at, to_at, values, transpose):
    spare = acc.shape[0] - 1
    slots = values.shape[0]
    live = facts[COUNT]
    contract = (((0,), (0,)), ((), ())) if transpose else (((1,), (0,)), ((), ()))

    def step(g, carry):
        base = g * GROUP
        products = [
            lax.dot_general(
                values[base + k], panel[facts[from_at + base + k]], contract, preferred_element_type=F32
            )
            for k in range(GROUP)
        ]
        for k in range(GROUP):
            to = jnp.where(base + k < live, facts[to_at + base + k], spare)
            acc[to] += products[k]
        return carry

    assert slots % GROUP == 0
    lax.fori_loop(0, (live + GROUP - 1) // GROUP, step, 0)


def keep_near_kernel(after, values, bias_0, bias_1, values_out, bias_0_out, bias_1_out):
    del after
    for source, target in ((values, values_out), (bias_0, bias_0_out), (bias_1, bias_1_out)):
        target[...] = source[...]


def first_kernel(facts, values, own, other, keep, send, panel, acc):
    fill_panel(panel, own, other, lax.rem(facts[PLACE_ROW], 2))
    acc[...] = jnp.zeros_like(acc)
    slots = values.shape[0]
    add_products(panel, acc, facts, FIRST + slots, FIRST, values, False)
    chips, half = keep.shape[:2]
    core = lax.rem(facts[PLACE_COL], 2)
    keep[...] = acc[:chips, pl.ds(pl.multiple_of(core * half, half), half), :]
    send[...] = acc[:chips, pl.ds(pl.multiple_of((1 - core) * half, half), half), :].astype(BF16)


def second_kernel(facts, values, own, other, keep, two, up, down, panel, acc):
    fill_panel(panel, own, other, lax.rem(facts[PLACE_COL], 2))
    acc[...] = jnp.zeros_like(acc)
    slots = values.shape[0]
    add_products(panel, acc, facts, FIRST, FIRST + slots, values, True)
    quads, half = keep.shape[:2]
    for ref, by in ((two, 2), (up, 1), (down, 3), (keep, 0)):
        r = lax.rem(facts[PLACE_ROW] + by, 4)
        offset = pl.multiple_of(lax.rem(r, 2) * half, half)
        for k in range(quads):
            ref[k] = acc[2 * k + r // 2, pl.ds(offset, half), :].astype(ref.dtype)


def dense_kernel(layer, parts, weight, bias, out):
    total = jnp.sum(parts[...].astype(F32), axis=0)
    high = total.astype(BF16)
    low = (total - high.astype(F32)).astype(BF16)
    result = jnp.dot(low, weight[...], preferred_element_type=F32)
    result += jnp.dot(high, weight[...], preferred_element_type=F32)
    result += bias[...]
    if layer == 0:
        result = jnp.maximum(result, 0.0)
    result = result.astype(BF16)
    if len(out.shape) == 3:
        for k in range(out.shape[0]):
            out[k] = result
    else:
        out[...] = result


def call(kernel, out_shape, in_specs, scratch=()):
    return pl.pallas_call(
        kernel,
        out_shape=out_shape,
        in_specs=in_specs,
        out_specs=jax.tree.map(lambda _: VMEM, out_shape),
        scratch_shapes=list(scratch),
        compiler_params=pltpu.CompilerParams(vmem_limit_bytes=VMEM_LIMIT),
    )


def shape(dims, dtype):
    return jax.ShapeDtypeStruct(dims, dtype)


def per_device(
    features,
    block_rows,
    block_cols,
    block_values,
    block_count,
    w_first,
    b_first,
    w_second,
    b_second,
):
    rows, cols = lax.axis_size(ROW), lax.axis_size(COL)
    own_rows, width = features.shape
    block = block_values.shape[-1]
    values = block_values[0, 0]
    row_blocks = own_rows * cols // block
    col_blocks = own_rows * rows // block
    scratch = (
        pltpu.VMEM((col_blocks, block, width), BF16),
        pltpu.VMEM((row_blocks + 1, block, width), F32),
    )
    place = jnp.stack([lax.axis_index(ROW), lax.axis_index(COL)]).astype(jnp.int32)
    facts = jnp.concatenate([place, block_count[0], block_rows[0, 0], block_cols[0, 0]])
    chips, quads = cols // 2, rows // 4

    same = lax.all_gather(features, ROW, axis_index_groups=strided(rows, 2))
    other = lax.ppermute(same, ROW, swap(rows))
    piece = (chips, own_rows, width)
    bias_shape = (1, width)
    near = (shape(values.shape, BF16), shape(bias_shape, F32), shape(bias_shape, F32))
    values, bias_first, bias_second = call(keep_near_kernel, near, [VMEM] * 4)(
        same, values, b_first.reshape(bias_shape), b_second.reshape(bias_shape)
    )
    keep, send = call(
        first_kernel, (shape(piece, F32), shape(piece, BF16)), [SMEM] + [VMEM] * 3, scratch
    )(facts, values, same, other)

    summed = (keep + lax.ppermute(send, COL, swap(cols)).astype(F32)).astype(BF16)
    terms = lax.all_to_all(summed, COL, 0, 0, axis_index_groups=strided(cols, 2))
    copies = call(functools.partial(dense_kernel, 0), shape(piece, BF16), [VMEM] * 3)(
        terms, w_first, bias_first
    )

    mine = lax.all_to_all(copies, COL, 0, 0, axis_index_groups=strided(cols, 2))
    other = lax.ppermute(mine, COL, swap(cols))
    piece = (quads, own_rows, width)
    keep, two, up, down = call(
        second_kernel,
        (shape(piece, F32), shape(piece, BF16), shape(piece, BF16), shape(piece, BF16)),
        [SMEM] + [VMEM] * 3,
        scratch,
    )(facts, values, mine, other)

    two = lax.ppermute(two, ROW, hop_two(rows))
    up = lax.ppermute(up, ROW, shift(rows, 1))
    down = lax.ppermute(down, ROW, shift(rows, -1))
    summed = (keep + two.astype(F32) + up.astype(F32) + down.astype(F32)).astype(BF16)
    terms = lax.all_to_all(summed, ROW, 0, 0, axis_index_groups=strided(rows, 4))
    return call(functools.partial(dense_kernel, 1), shape((own_rows, width), BF16), [VMEM] * 3)(
        terms, w_second, bias_second
    )


def solution(mesh):
    placed = (
        P((COL, ROW), None),
        P(ROW, COL, None),
        P(ROW, COL, None),
        P(ROW, COL, None, None, None),
        P(ROW, COL),
        P(),
        P(),
        P(),
        P(),
    )
    return jax.shard_map(
        per_device, mesh=mesh, in_specs=placed, out_specs=P((COL, ROW), None), check_vma=False
    )
```

```python
import functools

import jax
import jax.numpy as jnp
from jax import lax
from jax.experimental import pallas as pl
from jax.experimental.pallas import tpu as pltpu
from jax.sharding import PartitionSpec as P

ROW, COL = "row", "col"
BF16, F32 = jnp.bfloat16, jnp.float32
VMEM = pl.BlockSpec(memory_space=pltpu.VMEM)
SMEM = pl.BlockSpec(memory_space=pltpu.SMEM)
GROUP = 4
VMEM_LIMIT = 12 * 1024 * 1024
PLACE_ROW, PLACE_COL, COUNT, FIRST = 0, 1, 2, 3


def strided(size, stride):
    return [list(range(first, size, stride)) for first in range(stride)]


def shift(size, by):
    return [(i, (i + by) % size) for i in range(size)]


def hop_two(size):
    return [(i, (i + (-2 if i % 2 == 0 else 2)) % size) for i in range(size)]


def quartets(size):
    quads = size // 4
    return [[4 * j + (g if j < quads // 2 else g ^ 1) for j in range(quads)] for g in range(4)]


def swap(size):
    return [(i, i + 1 if i % 2 == 0 else i - 1) for i in range(size)]


def fill_panel(panel, own, other, side):
    half = own.shape[1]
    panel[:, pl.ds(pl.multiple_of(side * half, half), half), :] = own[...]
    panel[:, pl.ds(pl.multiple_of((1 - side) * half, half), half), :] = other[...]


def add_products(panel, acc, facts, from_at, to_at, values, transpose):
    spare = acc.shape[0] - 1
    slots = values.shape[0]
    live = facts[COUNT]
    contract = (((0,), (0,)), ((), ())) if transpose else (((1,), (0,)), ((), ()))

    def step(g, carry):
        base = g * GROUP
        products = [
            lax.dot_general(
                values[base + k], panel[facts[from_at + base + k]], contract, preferred_element_type=F32
            )
            for k in range(GROUP)
        ]
        for k in range(GROUP):
            to = jnp.where(base + k < live, facts[to_at + base + k], spare)
            acc[to] += products[k]
        return carry

    assert slots % GROUP == 0
    lax.fori_loop(0, (live + GROUP - 1) // GROUP, step, 0)


def keep_near_kernel(after, values, bias_0, bias_1, values_out, bias_0_out, bias_1_out):
    del after
    for source, target in ((values, values_out), (bias_0, bias_0_out), (bias_1, bias_1_out)):
        target[...] = source[...]


def first_kernel(facts, values, own, other, keep, send, panel, acc):
    fill_panel(panel, own, other, lax.rem(facts[PLACE_ROW], 2))
    acc[...] = jnp.zeros_like(acc)
    slots = values.shape[0]
    add_products(panel, acc, facts, FIRST + slots, FIRST, values, False)
    chips, half = keep.shape[:2]
    core = lax.rem(facts[PLACE_COL], 2)
    keep[...] = acc[:chips, pl.ds(pl.multiple_of(core * half, half), half), :]
    send[...] = acc[:chips, pl.ds(pl.multiple_of((1 - core) * half, half), half), :].astype(BF16)


def second_kernel(facts, values, own, other, keep, two, up, down, panel, acc):
    fill_panel(panel, own, other, lax.rem(facts[PLACE_COL], 2))
    acc[...] = jnp.zeros_like(acc)
    slots = values.shape[0]
    add_products(panel, acc, facts, FIRST, FIRST + slots, values, True)
    quads, half = keep.shape[:2]
    rows = 4 * quads
    z = facts[PLACE_ROW]
    odd = lax.rem(z, 2)
    for ref, to in ((two, z + 4 * odd - 2), (up, z + 1), (down, z - 1), (keep, z)):
        to = lax.rem(to + rows, rows)
        g = lax.rem(to, 4) ^ (to >= rows // 2).astype(jnp.int32)
        for j in range(quads):
            side = lax.rem(g + (0 if j < quads // 2 else 1), 2)
            offset = pl.multiple_of(side * half, half)
            ref[j] = acc[2 * j + g // 2, pl.ds(offset, half), :].astype(ref.dtype)


def dense_kernel(layer, parts, weight, bias, out):
    total = jnp.sum(parts[...].astype(F32), axis=0)
    high = total.astype(BF16)
    low = (total - high.astype(F32)).astype(BF16)
    result = jnp.dot(low, weight[...], preferred_element_type=F32)
    result += jnp.dot(high, weight[...], preferred_element_type=F32)
    result += bias[...]
    if layer == 0:
        result = jnp.maximum(result, 0.0)
    result = result.astype(BF16)
    if len(out.shape) == 3:
        for k in range(out.shape[0]):
            out[k] = result
    else:
        out[...] = result


def call(kernel, out_shape, in_specs, scratch=()):
    return pl.pallas_call(
        kernel,
        out_shape=out_shape,
        in_specs=in_specs,
        out_specs=jax.tree.map(lambda _: VMEM, out_shape),
        scratch_shapes=list(scratch),
        compiler_params=pltpu.CompilerParams(vmem_limit_bytes=VMEM_LIMIT),
    )


def shape(dims, dtype):
    return jax.ShapeDtypeStruct(dims, dtype)


def per_device(
    features,
    block_rows,
    block_cols,
    block_values,
    block_count,
    w_first,
    b_first,
    w_second,
    b_second,
):
    rows, cols = lax.axis_size(ROW), lax.axis_size(COL)
    own_rows, width = features.shape
    block = block_values.shape[-1]
    values = block_values[0, 0]
    row_blocks = own_rows * cols // block
    col_blocks = own_rows * rows // block
    scratch = (
        pltpu.VMEM((col_blocks, block, width), BF16),
        pltpu.VMEM((row_blocks + 1, block, width), F32),
    )
    place = jnp.stack([lax.axis_index(ROW), lax.axis_index(COL)]).astype(jnp.int32)
    facts = jnp.concatenate([place, block_count[0], block_rows[0, 0], block_cols[0, 0]])
    chips, quads = cols // 2, rows // 4

    same = lax.all_gather(features, ROW, axis_index_groups=strided(rows, 2))
    other = lax.ppermute(same, ROW, swap(rows))
    piece = (chips, own_rows, width)
    bias_shape = (1, width)
    near = (shape(values.shape, BF16), shape(bias_shape, F32), shape(bias_shape, F32))
    values, bias_first, bias_second = call(keep_near_kernel, near, [VMEM] * 4)(
        same, values, b_first.reshape(bias_shape), b_second.reshape(bias_shape)
    )
    keep, send = call(
        first_kernel, (shape(piece, F32), shape(piece, BF16)), [SMEM] + [VMEM] * 3, scratch
    )(facts, values, same, other)

    summed = (keep + lax.ppermute(send, COL, swap(cols)).astype(F32)).astype(BF16)
    terms = lax.all_to_all(summed, COL, 0, 0, axis_index_groups=strided(cols, 2))
    copies = call(functools.partial(dense_kernel, 0), shape(piece, BF16), [VMEM] * 3)(
        terms, w_first, bias_first
    )

    mine = lax.all_to_all(copies, COL, 0, 0, axis_index_groups=strided(cols, 2))
    other = lax.ppermute(mine, COL, swap(cols))
    piece = (quads, own_rows, width)
    keep, two, up, down = call(
        second_kernel,
        (shape(piece, F32), shape(piece, BF16), shape(piece, BF16), shape(piece, BF16)),
        [SMEM] + [VMEM] * 3,
        scratch,
    )(facts, values, mine, other)

    two = lax.ppermute(two, ROW, hop_two(rows))
    up = lax.ppermute(up, ROW, shift(rows, 1))
    down = lax.ppermute(down, ROW, shift(rows, -1))
    summed = (keep + two.astype(F32) + up.astype(F32) + down.astype(F32)).astype(BF16)
    terms = lax.all_to_all(summed, ROW, 0, 0, axis_index_groups=quartets(rows))
    return call(functools.partial(dense_kernel, 1), shape((own_rows, width), BF16), [VMEM] * 3)(
        terms, w_second, bias_second
    )


def solution(mesh):
    placed = (
        P((COL, ROW), None),
        P(ROW, COL, None),
        P(ROW, COL, None),
        P(ROW, COL, None, None, None),
        P(ROW, COL),
        P(),
        P(),
        P(),
        P(),
    )
    return jax.shard_map(
        per_device, mesh=mesh, in_specs=placed, out_specs=P((COL, ROW), None), check_vma=False
    )
```

```python
import jax
import jax.numpy as jnp
from jax import lax
from jax.experimental import pallas as pl
from jax.experimental.pallas import tpu as pltpu
from jax.sharding import PartitionSpec as P

ROW, COL = "row", "col"
BF16, F32 = jnp.bfloat16, jnp.float32
VMEM = pl.BlockSpec(memory_space=pltpu.VMEM)
SMEM = pl.BlockSpec(memory_space=pltpu.SMEM)
GROUP = 4
VMEM_LIMIT = 12 * 1024 * 1024
PLACE_ROW, PLACE_COL, COUNT, FIRST = 0, 1, 2, 3


def strided(size, stride):
    return [list(range(first, size, stride)) for first in range(stride)]


def shift(size, by):
    return [(i, (i + by) % size) for i in range(size)]


def hop_two(size):
    return [(i, (i + (2 if i % 2 == 0 else -2)) % size) for i in range(size)]


def swap(size):
    return [(i, i + 1 if i % 2 == 0 else i - 1) for i in range(size)]


def fill_panel(panel, own, other, side):
    half = own.shape[1]
    panel[:, pl.ds(pl.multiple_of(side * half, half), half), :] = own[...]
    panel[:, pl.ds(pl.multiple_of((1 - side) * half, half), half), :] = other[...]


def add_products(panel, acc, facts, from_at, to_at, values, transpose):
    spare = acc.shape[0] - 1
    slots = values.shape[0]
    live = facts[COUNT]
    contract = (((0,), (0,)), ((), ())) if transpose else (((1,), (0,)), ((), ()))

    def step(g, carry):
        base = g * GROUP
        products = [
            lax.dot_general(
                values[base + k], panel[facts[from_at + base + k]], contract, preferred_element_type=F32
            )
            for k in range(GROUP)
        ]
        for k in range(GROUP):
            to = jnp.where(base + k < live, facts[to_at + base + k], spare)
            acc[to] += products[k]
        return carry

    assert slots % GROUP == 0
    lax.fori_loop(0, (live + GROUP - 1) // GROUP, step, 0)


def keep_near_kernel(after, values, bias_0, bias_1, values_out, bias_0_out, bias_1_out):
    del after
    for source, target in ((values, values_out), (bias_0, bias_0_out), (bias_1, bias_1_out)):
        target[...] = source[...]


def first_kernel(facts, values, own, other, out, panel, acc):
    fill_panel(panel, own, other, lax.rem(facts[PLACE_ROW], 2))
    acc[...] = jnp.zeros_like(acc)
    slots = values.shape[0]
    add_products(panel, acc, facts, FIRST + slots, FIRST, values, False)
    out[...] = acc[: out.shape[0]].astype(BF16)


def split_kernel(facts, parts, keep, send, total):
    total[...] = jnp.sum(parts[...].astype(F32), axis=0)
    half = keep.shape[0]
    core = lax.rem(facts[PLACE_COL], 2)
    keep[...] = total[pl.ds(pl.multiple_of(core * half, half), half), :]
    send[...] = total[pl.ds(pl.multiple_of((1 - core) * half, half), half), :]


def second_kernel(facts, values, own, other, keep, two, up, down, panel, acc):
    fill_panel(panel, own, other, lax.rem(facts[PLACE_COL], 2))
    acc[...] = jnp.zeros_like(acc)
    slots = values.shape[0]
    add_products(panel, acc, facts, FIRST, FIRST + slots, values, True)
    quads, half = keep.shape[:2]
    for ref, by in ((two, 2), (up, 1), (down, 3), (keep, 0)):
        r = lax.rem(facts[PLACE_ROW] + by, 4)
        offset = pl.multiple_of(lax.rem(r, 2) * half, half)
        for k in range(quads):
            ref[k] = acc[2 * k + r // 2, pl.ds(offset, half), :].astype(ref.dtype)


def dense(total, weight, bias):
    high = total.astype(BF16)
    low = (total - high.astype(F32)).astype(BF16)
    result = jnp.dot(low, weight[...], preferred_element_type=F32)
    result += jnp.dot(high, weight[...], preferred_element_type=F32)
    return result + bias[...]


def hidden_kernel(keep, received, weight, bias, out):
    result = jnp.maximum(dense(keep[...] + received[...], weight, bias), 0.0).astype(BF16)
    for k in range(out.shape[0]):
        out[k] = result


def embed_kernel(parts, weight, bias, out):
    total = jnp.sum(parts[...].astype(F32), axis=0)
    out[...] = dense(total, weight, bias).astype(BF16)


def call(kernel, out_shape, in_specs, scratch=()):
    return pl.pallas_call(
        kernel,
        out_shape=out_shape,
        in_specs=in_specs,
        out_specs=jax.tree.map(lambda _: VMEM, out_shape),
        scratch_shapes=list(scratch),
        compiler_params=pltpu.CompilerParams(vmem_limit_bytes=VMEM_LIMIT),
    )


def shape(dims, dtype):
    return jax.ShapeDtypeStruct(dims, dtype)


def per_device(
    features,
    block_rows,
    block_cols,
    block_values,
    block_count,
    w_first,
    b_first,
    w_second,
    b_second,
):
    rows, cols = lax.axis_size(ROW), lax.axis_size(COL)
    own_rows, width = features.shape
    block = block_values.shape[-1]
    values = block_values[0, 0]
    row_blocks = own_rows * cols // block
    col_blocks = own_rows * rows // block
    scratch = (
        pltpu.VMEM((col_blocks, block, width), BF16),
        pltpu.VMEM((row_blocks + 1, block, width), F32),
    )
    place = jnp.stack([lax.axis_index(ROW), lax.axis_index(COL)]).astype(jnp.int32)
    facts = jnp.concatenate([place, block_count[0], block_rows[0, 0], block_cols[0, 0]])
    chips, quads = cols // 2, rows // 4

    same = lax.all_gather(features, ROW, axis_index_groups=strided(rows, 2))
    other = lax.ppermute(same, ROW, swap(rows))
    piece = (chips, own_rows, width)
    bias_shape = (1, width)
    near = (shape(values.shape, BF16), shape(bias_shape, F32), shape(bias_shape, F32))
    values, bias_first, bias_second = call(keep_near_kernel, near, [VMEM] * 4)(
        same, values, b_first.reshape(bias_shape), b_second.reshape(bias_shape)
    )
    partial_first = call(
        first_kernel, shape((chips, block, width), BF16), [SMEM] + [VMEM] * 3, scratch
    )(facts, values, same, other)

    terms = lax.all_to_all(partial_first, COL, 0, 0, axis_index_groups=strided(cols, 2))
    half = shape((own_rows, width), F32)
    keep, send = call(split_kernel, (half, half), [SMEM, VMEM], (pltpu.VMEM((block, width), F32),))(
        facts, terms
    )
    received = lax.ppermute(send, COL, swap(cols))
    copies = call(hidden_kernel, shape(piece, BF16), [VMEM] * 4)(keep, received, w_first, bias_first)

    mine = lax.all_to_all(copies, COL, 0, 0, axis_index_groups=strided(cols, 2))
    other = lax.ppermute(mine, COL, swap(cols))
    piece = (quads, own_rows, width)
    keep, two, up, down = call(
        second_kernel,
        (shape(piece, F32), shape(piece, BF16), shape(piece, BF16), shape(piece, BF16)),
        [SMEM] + [VMEM] * 3,
        scratch,
    )(facts, values, mine, other)

    two = lax.ppermute(two, ROW, hop_two(rows))
    up = lax.ppermute(up, ROW, shift(rows, 1))
    down = lax.ppermute(down, ROW, shift(rows, -1))
    summed = (keep + two.astype(F32) + up.astype(F32) + down.astype(F32)).astype(BF16)
    terms = lax.all_to_all(summed, ROW, 0, 0, axis_index_groups=strided(rows, 4))
    return call(embed_kernel, shape((own_rows, width), BF16), [VMEM] * 3)(
        terms, w_second, bias_second
    )


def solution(mesh):
    placed = (
        P((COL, ROW), None),
        P(ROW, COL, None),
        P(ROW, COL, None),
        P(ROW, COL, None, None, None),
        P(ROW, COL),
        P(),
        P(),
        P(),
        P(),
    )
    return jax.shard_map(
        per_device, mesh=mesh, in_specs=placed, out_specs=P((COL, ROW), None), check_vma=False
    )
```

```python
import functools

import jax
import jax.numpy as jnp
from jax import lax
from jax.experimental import pallas as pl
from jax.experimental.pallas import tpu as pltpu
from jax.sharding import PartitionSpec as P

ROW, COL = "row", "col"
BF16, F32 = jnp.bfloat16, jnp.float32
VMEM = pl.BlockSpec(memory_space=pltpu.VMEM)
SMEM = pl.BlockSpec(memory_space=pltpu.SMEM)
GROUP = 4
VMEM_LIMIT = 12 * 1024 * 1024
PLACE_ROW, PLACE_COL, COUNT, FIRST = 0, 1, 2, 3


def strided(size, stride):
    return [list(range(first, size, stride)) for first in range(stride)]


def shift(size, by):
    return [(i, (i + by) % size) for i in range(size)]


def hop_two(size):
    return [(i, (i + (-2 if i % 2 == 0 else 2)) % size) for i in range(size)]


def quartets(size):
    quads = size // 4
    return [
        [4 * j + (g if j < quads // 2 else g ^ 1) for j in reversed(range(quads))] for g in range(4)
    ]


def swap(size):
    return [(i, i + 1 if i % 2 == 0 else i - 1) for i in range(size)]


def fill_panel(panel, own, other, side):
    half = own.shape[1]
    panel[:, pl.ds(pl.multiple_of(side * half, half), half), :] = own[...]
    panel[:, pl.ds(pl.multiple_of((1 - side) * half, half), half), :] = other[...]


def add_products(panel, acc, facts, from_at, to_at, values, transpose):
    spare = acc.shape[0] - 1
    slots = values.shape[0]
    live = facts[COUNT]
    contract = (((0,), (0,)), ((), ())) if transpose else (((1,), (0,)), ((), ()))

    def step(g, carry):
        base = g * GROUP
        products = [
            lax.dot_general(
                values[base + k], panel[facts[from_at + base + k]], contract, preferred_element_type=F32
            )
            for k in range(GROUP)
        ]
        for k in range(GROUP):
            to = jnp.where(base + k < live, facts[to_at + base + k], spare)
            acc[to] += products[k]
        return carry

    assert slots % GROUP == 0
    lax.fori_loop(0, (live + GROUP - 1) // GROUP, step, 0)


def keep_near_kernel(after, values, bias_0, bias_1, values_out, bias_0_out, bias_1_out):
    del after
    for source, target in ((values, values_out), (bias_0, bias_0_out), (bias_1, bias_1_out)):
        target[...] = source[...]


def first_kernel(facts, values, own, other, keep, send, panel, acc):
    fill_panel(panel, own, other, lax.rem(facts[PLACE_ROW], 2))
    acc[...] = jnp.zeros_like(acc)
    slots = values.shape[0]
    add_products(panel, acc, facts, FIRST + slots, FIRST, values, False)
    chips, half = keep.shape[:2]
    core = lax.rem(facts[PLACE_COL], 2)
    keep[...] = acc[:chips, pl.ds(pl.multiple_of(core * half, half), half), :]
    send[...] = acc[:chips, pl.ds(pl.multiple_of((1 - core) * half, half), half), :].astype(BF16)


def second_kernel(facts, values, own, other, keep, two, up, down, panel, acc):
    fill_panel(panel, own, other, lax.rem(facts[PLACE_COL], 2))
    acc[...] = jnp.zeros_like(acc)
    slots = values.shape[0]
    add_products(panel, acc, facts, FIRST, FIRST + slots, values, True)
    quads, half = keep.shape[:2]
    rows = 4 * quads
    z = facts[PLACE_ROW]
    odd = lax.rem(z, 2)
    for ref, to in ((two, z + 4 * odd - 2), (up, z + 1), (down, z - 1), (keep, z)):
        to = lax.rem(to + rows, rows)
        g = lax.rem(to, 4) ^ (to >= rows // 2).astype(jnp.int32)
        for j in range(quads):
            side = lax.rem(g + (0 if j < quads // 2 else 1), 2)
            offset = pl.multiple_of(side * half, half)
            ref[quads - 1 - j] = acc[2 * j + g // 2, pl.ds(offset, half), :].astype(ref.dtype)


def dense_kernel(layer, parts, weight, bias, out):
    total = jnp.sum(parts[...].astype(F32), axis=0)
    high = total.astype(BF16)
    low = (total - high.astype(F32)).astype(BF16)
    result = jnp.dot(low, weight[...], preferred_element_type=F32)
    result += jnp.dot(high, weight[...], preferred_element_type=F32)
    result += bias[...]
    if layer == 0:
        result = jnp.maximum(result, 0.0)
    result = result.astype(BF16)
    if len(out.shape) == 3:
        for k in range(out.shape[0]):
            out[k] = result
    else:
        out[...] = result


def call(kernel, out_shape, in_specs, scratch=()):
    return pl.pallas_call(
        kernel,
        out_shape=out_shape,
        in_specs=in_specs,
        out_specs=jax.tree.map(lambda _: VMEM, out_shape),
        scratch_shapes=list(scratch),
        compiler_params=pltpu.CompilerParams(vmem_limit_bytes=VMEM_LIMIT),
    )


def shape(dims, dtype):
    return jax.ShapeDtypeStruct(dims, dtype)


def per_device(
    features,
    block_rows,
    block_cols,
    block_values,
    block_count,
    w_first,
    b_first,
    w_second,
    b_second,
):
    rows, cols = lax.axis_size(ROW), lax.axis_size(COL)
    own_rows, width = features.shape
    block = block_values.shape[-1]
    values = block_values[0, 0]
    row_blocks = own_rows * cols // block
    col_blocks = own_rows * rows // block
    scratch = (
        pltpu.VMEM((col_blocks, block, width), BF16),
        pltpu.VMEM((row_blocks + 1, block, width), F32),
    )
    place = jnp.stack([lax.axis_index(ROW), lax.axis_index(COL)]).astype(jnp.int32)
    facts = jnp.concatenate([place, block_count[0], block_rows[0, 0], block_cols[0, 0]])
    chips, quads = cols // 2, rows // 4

    same = lax.all_gather(features, ROW, axis_index_groups=strided(rows, 2))
    other = lax.ppermute(same, ROW, swap(rows))
    piece = (chips, own_rows, width)
    bias_shape = (1, width)
    near = (shape(values.shape, BF16), shape(bias_shape, F32), shape(bias_shape, F32))
    values, bias_first, bias_second = call(keep_near_kernel, near, [VMEM] * 4)(
        same, values, b_first.reshape(bias_shape), b_second.reshape(bias_shape)
    )
    keep, send = call(
        first_kernel, (shape(piece, F32), shape(piece, BF16)), [SMEM] + [VMEM] * 3, scratch
    )(facts, values, same, other)

    summed = (keep + lax.ppermute(send, COL, swap(cols)).astype(F32)).astype(BF16)
    terms = lax.all_to_all(summed, COL, 0, 0, axis_index_groups=strided(cols, 2))
    copies = call(functools.partial(dense_kernel, 0), shape(piece, BF16), [VMEM] * 3)(
        terms, w_first, bias_first
    )

    mine = lax.all_to_all(copies, COL, 0, 0, axis_index_groups=strided(cols, 2))
    other = lax.ppermute(mine, COL, swap(cols))
    piece = (quads, own_rows, width)
    keep, two, up, down = call(
        second_kernel,
        (shape(piece, F32), shape(piece, BF16), shape(piece, BF16), shape(piece, BF16)),
        [SMEM] + [VMEM] * 3,
        scratch,
    )(facts, values, mine, other)

    two = lax.ppermute(two, ROW, hop_two(rows))
    up = lax.ppermute(up, ROW, shift(rows, 1))
    down = lax.ppermute(down, ROW, shift(rows, -1))
    summed = (keep + two.astype(F32) + up.astype(F32) + down.astype(F32)).astype(BF16)
    terms = lax.all_to_all(summed, ROW, 0, 0, axis_index_groups=quartets(rows))
    return call(functools.partial(dense_kernel, 1), shape((own_rows, width), BF16), [VMEM] * 3)(
        terms, w_second, bias_second
    )


def solution(mesh):
    placed = (
        P((COL, ROW), None),
        P(ROW, COL, None),
        P(ROW, COL, None),
        P(ROW, COL, None, None, None),
        P(ROW, COL),
        P(),
        P(),
        P(),
        P(),
    )
    return jax.shard_map(
        per_device, mesh=mesh, in_specs=placed, out_specs=P((COL, ROW), None), check_vma=False
    )
```

```python
import functools

import jax
import jax.numpy as jnp
from jax import lax
from jax.experimental import pallas as pl
from jax.experimental.pallas import tpu as pltpu
from jax.sharding import PartitionSpec as P

ROW, COL = "row", "col"
BF16, F32 = jnp.bfloat16, jnp.float32
VMEM = pl.BlockSpec(memory_space=pltpu.VMEM)
SMEM = pl.BlockSpec(memory_space=pltpu.SMEM)
GROUP = 4
VMEM_LIMIT = 12 * 1024 * 1024
PLACE_ROW, PLACE_COL, COUNT, FIRST = 0, 1, 2, 3


def strided(size, stride):
    return [list(range(first, size, stride)) for first in range(stride)]


def shift(size, by):
    return [(i, (i + by) % size) for i in range(size)]


def hop_two(size):
    return [(i, (i + (-2 if i % 2 == 0 else 2)) % size) for i in range(size)]


def quartets(size):
    quads = size // 4
    return [
        [4 * j + (g if j < quads // 2 else g ^ 1) for j in range(quads)][:: 1 if g % 2 else -1]
        for g in range(4)
    ]


def swap(size):
    return [(i, i + 1 if i % 2 == 0 else i - 1) for i in range(size)]


def fill_panel(panel, own, other, side):
    half = own.shape[1]
    panel[:, pl.ds(pl.multiple_of(side * half, half), half), :] = own[...]
    panel[:, pl.ds(pl.multiple_of((1 - side) * half, half), half), :] = other[...]


def add_products(panel, acc, facts, from_at, to_at, values, transpose):
    spare = acc.shape[0] - 1
    slots = values.shape[0]
    live = facts[COUNT]
    contract = (((0,), (0,)), ((), ())) if transpose else (((1,), (0,)), ((), ()))

    def step(g, carry):
        base = g * GROUP
        products = [
            lax.dot_general(
                values[base + k], panel[facts[from_at + base + k]], contract, preferred_element_type=F32
            )
            for k in range(GROUP)
        ]
        for k in range(GROUP):
            to = jnp.where(base + k < live, facts[to_at + base + k], spare)
            acc[to] += products[k]
        return carry

    assert slots % GROUP == 0
    lax.fori_loop(0, (live + GROUP - 1) // GROUP, step, 0)


def keep_near_kernel(after, values, bias_0, bias_1, values_out, bias_0_out, bias_1_out):
    del after
    for source, target in ((values, values_out), (bias_0, bias_0_out), (bias_1, bias_1_out)):
        target[...] = source[...]


def first_kernel(facts, values, own, other, keep, send, panel, acc):
    fill_panel(panel, own, other, lax.rem(facts[PLACE_ROW], 2))
    acc[...] = jnp.zeros_like(acc)
    slots = values.shape[0]
    add_products(panel, acc, facts, FIRST + slots, FIRST, values, False)
    chips, half = keep.shape[:2]
    core = lax.rem(facts[PLACE_COL], 2)
    keep[...] = acc[:chips, pl.ds(pl.multiple_of(core * half, half), half), :]
    send[...] = acc[:chips, pl.ds(pl.multiple_of((1 - core) * half, half), half), :].astype(BF16)


def second_kernel(facts, values, own, other, keep, two, up, down, panel, acc):
    fill_panel(panel, own, other, lax.rem(facts[PLACE_COL], 2))
    acc[...] = jnp.zeros_like(acc)
    slots = values.shape[0]
    add_products(panel, acc, facts, FIRST, FIRST + slots, values, True)
    quads, half = keep.shape[:2]
    rows = 4 * quads
    z = facts[PLACE_ROW]
    odd = lax.rem(z, 2)
    for ref, to in ((two, z + 4 * odd - 2), (up, z + 1), (down, z - 1), (keep, z)):
        to = lax.rem(to + rows, rows)
        g = lax.rem(to, 4) ^ (to >= rows // 2).astype(jnp.int32)
        for j in range(quads):
            side = lax.rem(g + (0 if j < quads // 2 else 1), 2)
            offset = pl.multiple_of(side * half, half)
            slot = jnp.where(lax.rem(g, 2) == 0, quads - 1 - j, j)
            ref[slot] = acc[2 * j + g // 2, pl.ds(offset, half), :].astype(ref.dtype)


def dense_kernel(layer, parts, weight, bias, out):
    total = jnp.sum(parts[...].astype(F32), axis=0)
    high = total.astype(BF16)
    low = (total - high.astype(F32)).astype(BF16)
    result = jnp.dot(low, weight[...], preferred_element_type=F32)
    result += jnp.dot(high, weight[...], preferred_element_type=F32)
    result += bias[...]
    if layer == 0:
        result = jnp.maximum(result, 0.0)
    result = result.astype(BF16)
    if len(out.shape) == 3:
        for k in range(out.shape[0]):
            out[k] = result
    else:
        out[...] = result


def call(kernel, out_shape, in_specs, scratch=()):
    return pl.pallas_call(
        kernel,
        out_shape=out_shape,
        in_specs=in_specs,
        out_specs=jax.tree.map(lambda _: VMEM, out_shape),
        scratch_shapes=list(scratch),
        compiler_params=pltpu.CompilerParams(vmem_limit_bytes=VMEM_LIMIT),
    )


def shape(dims, dtype):
    return jax.ShapeDtypeStruct(dims, dtype)


def per_device(
    features,
    block_rows,
    block_cols,
    block_values,
    block_count,
    w_first,
    b_first,
    w_second,
    b_second,
):
    rows, cols = lax.axis_size(ROW), lax.axis_size(COL)
    own_rows, width = features.shape
    block = block_values.shape[-1]
    values = block_values[0, 0]
    row_blocks = own_rows * cols // block
    col_blocks = own_rows * rows // block
    scratch = (
        pltpu.VMEM((col_blocks, block, width), BF16),
        pltpu.VMEM((row_blocks + 1, block, width), F32),
    )
    place = jnp.stack([lax.axis_index(ROW), lax.axis_index(COL)]).astype(jnp.int32)
    facts = jnp.concatenate([place, block_count[0], block_rows[0, 0], block_cols[0, 0]])
    chips, quads = cols // 2, rows // 4

    same = lax.all_gather(features, ROW, axis_index_groups=strided(rows, 2))
    other = lax.ppermute(same, ROW, swap(rows))
    piece = (chips, own_rows, width)
    bias_shape = (1, width)
    near = (shape(values.shape, BF16), shape(bias_shape, F32), shape(bias_shape, F32))
    values, bias_first, bias_second = call(keep_near_kernel, near, [VMEM] * 4)(
        same, values, b_first.reshape(bias_shape), b_second.reshape(bias_shape)
    )
    keep, send = call(
        first_kernel, (shape(piece, F32), shape(piece, BF16)), [SMEM] + [VMEM] * 3, scratch
    )(facts, values, same, other)

    summed = (keep + lax.ppermute(send, COL, swap(cols)).astype(F32)).astype(BF16)
    terms = lax.all_to_all(summed, COL, 0, 0, axis_index_groups=strided(cols, 2))
    copies = call(functools.partial(dense_kernel, 0), shape(piece, BF16), [VMEM] * 3)(
        terms, w_first, bias_first
    )

    mine = lax.all_to_all(copies, COL, 0, 0, axis_index_groups=strided(cols, 2))
    other = lax.ppermute(mine, COL, swap(cols))
    piece = (quads, own_rows, width)
    keep, two, up, down = call(
        second_kernel,
        (shape(piece, F32), shape(piece, BF16), shape(piece, BF16), shape(piece, BF16)),
        [SMEM] + [VMEM] * 3,
        scratch,
    )(facts, values, mine, other)

    two = lax.ppermute(two, ROW, hop_two(rows))
    up = lax.ppermute(up, ROW, shift(rows, 1))
    down = lax.ppermute(down, ROW, shift(rows, -1))
    summed = (keep + two.astype(F32) + up.astype(F32) + down.astype(F32)).astype(BF16)
    terms = lax.all_to_all(summed, ROW, 0, 0, axis_index_groups=quartets(rows))
    return call(functools.partial(dense_kernel, 1), shape((own_rows, width), BF16), [VMEM] * 3)(
        terms, w_second, bias_second
    )


def solution(mesh):
    placed = (
        P((COL, ROW), None),
        P(ROW, COL, None),
        P(ROW, COL, None),
        P(ROW, COL, None, None, None),
        P(ROW, COL),
        P(),
        P(),
        P(),
        P(),
    )
    return jax.shard_map(
        per_device, mesh=mesh, in_specs=placed, out_specs=P((COL, ROW), None), check_vma=False
    )
```
